128 devices in a mesh: dp: 16 (over x_lo, y, core), fsdp: 8 (over z, x_hi).
Axes of the slice: x: 4 (x_hi: 2, x_lo: 2; x = x_hi * 2 + x_lo), y: 4, z: 4, core: 2. Of those that a mesh axis runs over, the one named last changes fastest.
Arguments:
- tokens: bfloat16 [65536, 8192], P(('dp', 'fsdp')), may hold values from -24 to 24
- out_grad: bfloat16 [65536, 1024], P(('dp', 'fsdp')), may hold values from -0.5 to 0.5
- weight_codes: bfloat16 [8192, 1024], P('fsdp'), may hold values from -127 to 127
- block_scales: float32 [8192, 8], P('fsdp'), may hold values from 0.003 to 0.03
- proj_basis: bfloat16 [1024, 512], replicated, may hold values from -0.1875 to 0.1875
- first_prev: float32 [8192, 512], P('fsdp', 'dp'), may hold values from -6 to 6
- second_prev: float32 [8192, 512], P('fsdp', 'dp'), may hold values from 0.5 to 4
Outputs:
- input_grad: bfloat16 [65536, 8192], P(('dp', 'fsdp'))
- first_new: float32 [8192, 512], P('fsdp', 'dp')
- second_new: float32 [8192, 512], P('fsdp', 'dp')
- new_weight: bfloat16 [8192, 1024], P('fsdp')
The draws below stay inside these ranges and needn't reach their ends.
All inputs are finite; a program needn't handle non-finite values.
Results may differ from the reference program's by a relative error of at most 0.015.
Values may be sent and summed in bfloat16 or wider, within the bound.
A program may use at most 128 MiB of HBM per device.

```python
import math
import jax
import jax.numpy as jnp
from jax import lax

D = 8192
N = 1024
RANK = 512
BLOCK = 128
TOKENS = 65536


def raised(values, rng, source, target, parts, factor):
    def block_of(dim):
        return (jnp.arange(values.shape[dim]) // (values.shape[dim] // parts)).reshape((-1,) + (1,) * (values.ndim - 1 - dim))

    first = jax.random.permutation(rng, parts)[block_of(target)]
    other_side = (block_of(target) + parts // 2) % parts
    return jnp.where((block_of(source) == first) | (block_of(source) == other_side), factor * values, values)


def shard_levels(stream_key, shape, shards, low, top_value):
    def one(axis_at, blocks):
        draws = jax.random.uniform(jax.random.fold_in(jax.random.fold_in(stream_key, 6), axis_at), (blocks,), jnp.float32, low / len(shards), top_value / len(shards))
        return jnp.repeat(jnp.exp(draws), shape[axis_at] // blocks).reshape((-1,) + (1,) * (len(shape) - axis_at - 1))

    level = one(*shards[0])
    for cut in shards[1:]:
        level = level * one(*cut)
    return level


def scatter_about(rng, extent, spread, most, shards=(), held_as=jnp.bfloat16):
    gain = shard_levels(rng, extent, shards, -0.22, 0.18) if shards else 1.0
    drawn = jax.random.normal(rng, extent, jnp.float32) * spread * gain
    return jnp.minimum(jnp.maximum(drawn, -most), most).astype(held_as)


def noise_with(own_key, extent, width, most, cuts, heavy, kind=jnp.bfloat16):
    entries = width * jax.random.normal(own_key, extent, jnp.float32)
    if cuts:
        entries = entries * shard_levels(own_key, extent, cuts, -0.22, 0.18)
    return jnp.clip(raised(entries, jax.random.fold_in(own_key, 3), *heavy), -most, most).astype(kind)


def setup_inputs(seed: int = 0) -> dict:
    key_of = jax.random.split(jax.random.key(seed), 8)
    tokens = noise_with(key_of[0], (TOKENS, D), 1.0, 24.0, ((0, 128),), (0, 1, 128, 5.5))
    out_grad = scatter_about(key_of[1], (TOKENS, N), (N ** -0.5), 0.5, ((0, 128),))
    weight_codes = jnp.clip(jax.random.uniform(key_of[2], (D, N), jnp.float32, -127.0, 127.0) * shard_levels(key_of[2], (D, N), ((0, 8),), -0.4, 0.0), -127.0, 127.0).astype(jnp.bfloat16)
    block_scales = jnp.clip(jnp.exp(math.log(0.03) - 2.3025851 * jax.random.uniform(key_of[3], (D, N // BLOCK), jnp.float32) ** shard_levels(key_of[3], (D, N // BLOCK), ((0, 8),), -0.2, 0.2)), 0.003, 0.03)
    proj_basis = scatter_about(key_of[4], (N, RANK), N ** -0.5, 0.1875)
    first_prev = scatter_about(key_of[5], (D, RANK), 1.0, 6.0, ((0, 8), (1, 16)), jnp.float32)
    second_prev = jnp.clip(jnp.exp(math.log(4.0) - 2.0794415 * jax.random.uniform(key_of[6], (D, RANK), jnp.float32) ** shard_levels(key_of[6], (D, RANK), ((0, 8), (1, 16)), -0.2, 0.2)), 0.5, 4.0)
    return {"tokens": tokens, "out_grad": out_grad, "weight_codes": weight_codes, "block_scales": block_scales, "proj_basis": proj_basis, "first_prev": first_prev, "second_prev": second_prev}


beta_one = 0.9
beta_two = 0.999
learn_rate = 0.2
epsilon = 1e-08

def reference(tokens, out_grad, weight_codes, block_scales, proj_basis, first_prev, second_prev):
    blocks = weight_codes.reshape(D, N // BLOCK, BLOCK).astype(jnp.float32) * block_scales[:, :, None]
    weight = blocks.reshape(D, N).astype(jnp.bfloat16)
    input_grad = lax.dot_general(out_grad, weight, (((1,), (1,)), ((), ())), preferred_element_type=jnp.float32).astype(jnp.bfloat16)
    projected = jnp.dot(out_grad, proj_basis, preferred_element_type=jnp.float32).astype(jnp.bfloat16)
    low_grad = lax.dot_general(tokens, projected, (((0,), (0,)), ((), ())), preferred_element_type=jnp.float32)
    first_new = beta_one * first_prev + (1.0 - beta_one) * low_grad
    second_new = beta_two * second_prev + (1.0 - beta_two) * low_grad * low_grad
    step_low = (first_new / (jnp.sqrt(second_new) + epsilon)).astype(jnp.bfloat16)
    change = lax.dot_general(step_low, proj_basis, (((1,), (1,)), ((), ())), preferred_element_type=jnp.float32)
    new_weight = (weight.astype(jnp.float32) - learn_rate * change).astype(jnp.bfloat16)
    return (input_grad, first_new, second_new, new_weight)
```

```python
import functools

import jax
import jax.numpy as jnp
from jax import lax
from jax.experimental import pallas as pl
from jax.experimental.pallas import tpu as pltpu
from jax.sharding import PartitionSpec as P

MESH = pl.DeviceIdType.MESH
BF16 = jnp.bfloat16
F32 = jnp.float32
beta_one = 0.9
beta_two = 0.999
learn_rate = 0.2
epsilon = 1e-08

D = 8192
N = 1024
RANK = 512
TOK = 512
LAG = 2
NT = (((1,), (1,)), ((), ()))


class Net:
    def __init__(self, send_sems, recv_sems):
        self.send_sems, self.recv_sems = send_sems, recv_sems
        self.table = {}
        self.sent, self.got = set(), set()

    def start(self, name, src, dst, device):
        at = len(self.table)
        copy = pltpu.make_async_remote_copy(
            src_ref=src,
            dst_ref=dst,
            send_sem=self.send_sems.at[at],
            recv_sem=self.recv_sems.at[at],
            device_id=device,
            device_id_type=MESH,
        )
        self.table[name] = copy
        copy.start()

    def recv(self, name):
        if name not in self.got:
            self.got.add(name)
            self.table[name].wait_recv()

    def finish(self):
        for name, copy in self.table.items():
            self.recv(name)
        for name, copy in self.table.items():
            copy.wait_send()


COPIES = 128


def exchange(
    tokens, out_grad, codes, scales, basis, first_prev, second_prev,
    ig, step_all, first_new, second_new, weight,
    W, og, stage, cod, sca, bas, tok, proj_t, sib_out, sib_in, own, cs, rr, s2, y_in, cs2, x_in, z_out, z_in,
    fp, sp, send_sems, recv_sems, load_sems,
):
    d = lax.axis_index("dp")
    f = lax.axis_index("fsdp")
    xlo, y, c = d // 8, (d // 2) % 4, d % 2
    z, xhi = f // 2, f % 2

    def dev(dx=0, dh=0, dy=0, dz=0, dc=0):
        xl = 1 - xlo if dx else xlo
        xh = 1 - xhi if dh else xhi
        cc = 1 - c if dc else c
        return (xl * 8 + ((y + dy) % 4) * 2 + cc, ((z + dz) % 4) * 2 + xh)

    sib = dev(dc=1)
    zp, zm = dev(dz=1), dev(dz=3)
    yp, ym = dev(dy=1), dev(dy=3)
    xc, xs, xo = dev(dx=1, dh=1), dev(dx=1), dev(dh=1)
    peers = [sib, zp, zm, dev(dz=2), xc, xs, xo] + [dev(dx=j // 4, dy=j % 4) for j in (1, 2, 3, 5, 6, 7)]

    loads = {}

    def load(name, src, dst):
        copy = pltpu.make_async_copy(src, dst, load_sems.at[len(loads)])
        loads[name] = copy
        copy.start()

    half = pl.multiple_of(c * 512, 512)
    other = pl.multiple_of(512 - c * 512, 512)
    load("scales", scales, sca)
    load("own_codes", codes.at[pl.ds(half, 512)], cod.at[pl.ds(half, 512)])
    load("og", out_grad, og.at[0])
    load("basis", basis, bas)

    def token_columns(q):
        return pl.multiple_of((((z + 1 + q // 2) % 4) * 2 + q % 2) * 1024, 1024)

    def load_tokens(q):
        load(("tok", q), tokens.at[:, pl.ds(token_columns(q), 1024)], tok.at[q % 4])

    for q in range(4):
        load_tokens(q)
    load("other_codes", codes.at[pl.ds(other, 512)], cod.at[pl.ds(other, 512)])
    load("fp", first_prev, fp)
    load("sp", second_prev, sp)

    barrier = pltpu.get_barrier_semaphore()
    for peer in peers:
        pl.semaphore_signal(barrier, inc=1, device_id=peer, device_id_type=MESH)

    def dequantize(base, also):
        def tile(i, carry):
            rows = pl.multiple_of(base + i * 128, 128)
            s = jnp.transpose(sca[:, pl.ds(rows, 128)])
            for g in range(8):
                cols = slice(g * 128, (g + 1) * 128)
                w = (cod[pl.ds(rows, 128), cols].astype(F32) * s[:, g : g + 1]).astype(BF16)
                weight[pl.ds(rows, 128), cols] = w
                if also:
                    W[0, pl.ds(pl.multiple_of(i * 128, 128), 128), cols] = w
            return carry

        lax.fori_loop(0, 4, tile, 0)

    loads["scales"].wait()
    loads["own_codes"].wait()
    dequantize(half, True)

    pl.semaphore_wait(barrier, len(peers))
    net = Net(send_sems, recv_sems)

    def wsend(name, way, dz, h, start, size):
        device, to_dz, to_h = {
            "z+": (zp, (dz + 3) % 4, h),
            "z-": (zm, (dz + 1) % 4, h),
            "xc": (xc, dz, 1 - h),
            "xs": (xs, dz, h),
        }[way]
        if not isinstance(start, int):
            start = pl.multiple_of(start, 64)
        rows = pl.ds(start, size)
        net.start(name, W.at[dz * 2 + h, rows], W.at[to_dz * 2 + to_h, rows], device)

    wsend("zp1a", "z+", 0, 0, 0, 256)
    wsend("zm1a", "z-", 0, 0, 256, 256)
    wsend("xc0", "xc", 0, 0, xlo * 256, 256)
    loads["og"].wait()
    net.start("og", og.at[0], og.at[1], sib)
    wsend("zp1b", "z+", 0, 0, 256, 256)
    wsend("zm1b", "z-", 0, 0, 0, 256)

    loads["basis"].wait()
    projected = jnp.dot(og[0], bas[...], preferred_element_type=F32).astype(BF16)
    turned = jnp.transpose(projected)
    for j in range(16):
        jx, jy, jc = j // 8, (j // 2) % 4, j % 2
        row = jnp.where(c == jc, 0, 256) + ((jy - y + 4) % 4) * 64 + jx * 32
        proj_t[pl.ds(pl.multiple_of(row, 32), 32), :] = turned[j * 32 : (j + 1) * 32, :]

    def partial_sums(q):
        loads["tok", q].wait()

        def tile(i, carry):
            cols = pl.ds(pl.multiple_of(i * 256, 256), 256)
            acc = jnp.dot(proj_t[...], tok[q % 4, :, cols], preferred_element_type=F32)
            own[q % (LAG + 1), :, cols] = acc[:256]
            sib_out[q, :, cols] = acc[256:].astype(BF16)
            return carry

        lax.fori_loop(0, 4, tile, 0)
        net.start(("sib", q), sib_out.at[q], sib_in.at[q], sib)
        if q + 4 < 8:
            load_tokens(q + 4)

    def chip_sums(q):
        net.recv(("sib", q))

        def tile(i, carry):
            rows = pl.ds(pl.multiple_of(i * 64, 64), 64)
            cs[q, rows, :] = (own[q % (LAG + 1), rows, :] + sib_in[q, rows, :].astype(F32)).astype(BF16)
            return carry

        lax.fori_loop(0, 4, tile, 0)
        net.start(("far", q), cs.at[q, pl.ds(128, 64)], rr.at[q], (yp, ym)[q % 2])

    def relay(q):
        net.recv(("far", q))
        near, direct = ((64, 192), (192, 64))[q % 2]
        s2[q] = (cs[q, near : near + 64, :].astype(F32) + rr[q].astype(F32)).astype(BF16)
        net.start(("near", q), s2.at[q], y_in.at[q, q % 2], (yp, ym)[q % 2])
        net.start(("direct", q), cs.at[q, pl.ds(direct, 64)], y_in.at[q, 1 - q % 2], (ym, yp)[q % 2])

    def y_sums(k):
        for h in range(2):
            q = 2 * k + h
            net.recv(("near", q))
            net.recv(("direct", q))
            cs2[k, h] = (cs[q, 0:64, :].astype(F32) + y_in[q, 0].astype(F32) + y_in[q, 1].astype(F32)).astype(BF16)
        for n, (to, xl, xh) in enumerate(((xc, 1 - xlo, 1 - xhi), (xs, 1 - xlo, xhi), (xo, xlo, 1 - xhi))):
            rows = pl.ds(pl.multiple_of(xl * 32, 32), 32)
            net.start(("x", k, n), cs2.at[k, xh, rows], x_in.at[k, n], to)

    def x_sums(k):
        total = cs2[k, xhi, pl.ds(pl.multiple_of(xlo * 32, 32), 32), :].astype(F32)
        for n in range(3):
            net.recv(("x", k, n))
            total = total + x_in[k, n].astype(F32)
        if k < 3:
            z_out[k] = total.astype(BF16)
            net.start(("z", k), z_out.at[k], z_in.at[k], dev(dz=1 + k))
        return total

    def product(dz, h, u):
        slot = dz * 2 + h
        fsdp = ((z + dz) % 4) * 2 + (xhi if h == 0 else 1 - xhi)
        cols = pl.ds(pl.multiple_of(fsdp * 1024 + c * 512 + u * 256, 256), 256)

        def tile(i, carry):
            rows = pl.ds(pl.multiple_of(i * 256, 256), 256)
            w = W[slot, u * 256 : (u + 1) * 256, :]
            mine = lax.dot_general(og[0, rows, :], w, NT, preferred_element_type=F32)
            ig[rows, cols] = mine.astype(BF16)
            theirs = lax.dot_general(og[1, rows, :], w, NT, preferred_element_type=F32)
            stage[slot, u, rows, :] = theirs.astype(BF16)
            return carry

        lax.fori_loop(0, 2, tile, 0)
        net.start(("ig", slot, u), stage.at[slot, u], ig.at[:, cols], sib)

    for q in range(8):
        partial_sums(q)
        if q >= LAG:
            chip_sums(q - LAG)
    for q in range(8 - LAG, 8):
        chip_sums(q)
    for q in range(4):
        relay(q)
    net.recv("og")
    product(0, 0, 0)
    product(0, 0, 1)

    net.recv("zp1a")
    wsend("zp2", "z+", 3, 0, 0, 256)
    wsend("xc3a", "xc", 3, 0, 128 + xlo * 64, 64)
    net.recv("zm1a")
    wsend("zm2", "z-", 1, 0, 256, 256)
    wsend("xc1a", "xc", 1, 0, 256 + xlo * 64, 64)
    net.recv("xc0")
    wsend("xs0", "xs", 0, 1, (1 - xlo) * 256, 256)
    for q in range(4, 8):
        relay(q)
    product(3, 0, 0)
    product(1, 0, 1)
    loads["other_codes"].wait()
    dequantize(other, False)
    y_sums(0)

    net.recv("zp1b")
    wsend("xc3b", "xc", 3, 0, 256 + xlo * 128, 128)
    net.recv("zm1b")
    wsend("xc1b", "xc", 1, 0, xlo * 128, 128)
    net.recv("xc3a")
    wsend("xs3a", "xs", 3, 1, 128 + (1 - xlo) * 64, 64)
    net.recv("xc1a")
    wsend("xs1a", "xs", 1, 1, 256 + (1 - xlo) * 64, 64)
    net.recv("xs0")
    wsend("zp_o1", "z+", 0, 1, 0, 128)
    wsend("zm_o1", "z-", 0, 1, 384, 128)
    x_sums(0)
    product(3, 0, 1)
    product(1, 0, 0)
    product(0, 1, 0)
    product(0, 1, 1)
    y_sums(1)

    net.recv("zp2")
    wsend("xc2a", "xc", 2, 0, 128 + xlo * 64, 64)
    net.recv("zm2")
    wsend("xc2b", "xc", 2, 0, 256 + xlo * 64, 64)
    x_sums(1)
    y_sums(2)
    net.recv("zp_o1")
    wsend("zp_o2", "z+", 3, 1, 0, 128)
    net.recv("zm_o1")
    wsend("zm_o2", "z-", 1, 1, 384, 128)
    net.recv("xc3b")
    wsend("xs3b", "xs", 3, 1, 256 + (1 - xlo) * 128, 128)
    net.recv("xc1b")
    wsend("xs1b", "xs", 1, 1, (1 - xlo) * 128, 128)
    product(2, 0, 0)
    product(2, 0, 1)
    x_sums(2)
    y_sums(3)
    net.recv("xs3a")
    product(3, 1, 0)
    net.recv("xs1a")
    product(1, 1, 1)
    low = x_sums(3)
    for k in range(3):
        net.recv(("z", k))
        low = low + z_in[k].astype(F32)

    loads["fp"].wait()
    loads["sp"].wait()
    first = beta_one * fp[...] + (1.0 - beta_one) * low
    second = beta_two * sp[...] + (1.0 - beta_two) * low * low
    first_new[...] = first
    second_new[...] = second
    mine = pl.ds(pl.multiple_of(d * 32, 32), 32)
    step_all[mine, :] = (first / (jnp.sqrt(second) + epsilon)).astype(BF16)
    for j in range(1, 8):
        net.start(("step", j), step_all.at[mine], step_all.at[mine], dev(dx=j // 4, dy=j % 4))
    net.start(("step_sib", 0), step_all.at[mine], step_all.at[mine], sib)

    net.recv("xc2a")
    wsend("xs2a", "xs", 2, 1, 128 + (1 - xlo) * 64, 64)
    net.recv("xc2b")
    wsend("xs2b", "xs", 2, 1, 256 + (1 - xlo) * 64, 64)
    net.recv("xs3b")
    product(3, 1, 1)
    net.recv("xs1b")
    product(1, 1, 0)
    for j in range(1, 8):
        net.recv(("step", j))
        xl = 1 - xlo if j // 4 else xlo
        rows = pl.ds(pl.multiple_of((xl * 8 + ((y - j % 4 + 4) % 4) * 2 + c) * 32, 32), 32)
        net.start(("step_sib", j), step_all.at[rows], step_all.at[rows], sib)
    net.recv("zp_o2")
    net.recv("xs2a")
    product(2, 1, 0)
    net.recv("zm_o2")
    net.recv("xs2b")
    product(2, 1, 1)
    net.finish()


def write_out(ig, step_all, first_new, second_new, weight, basis, ig_out, first_out, second_out, weight_out, nw, sems):
    copies = [
        pltpu.make_async_copy(ig.at[pl.ds(i * 128, 128)], ig_out.at[pl.ds(i * 128, 128)], sems.at[i]) for i in range(4)
    ]
    copies.append(pltpu.make_async_copy(first_new, first_out, sems.at[4]))
    copies.append(pltpu.make_async_copy(second_new, second_out, sems.at[5]))
    for copy in copies:
        copy.start()
    for i in range(4):
        rows = slice(i * 256, (i + 1) * 256)
        step = jnp.transpose(step_all[:, rows])
        change = lax.dot_general(step, basis[...], NT, preferred_element_type=F32)
        nw[rows, :] = (weight[rows, :].astype(F32) - learn_rate * change).astype(BF16)
        copy = pltpu.make_async_copy(nw.at[pl.ds(i * 256, 256)], weight_out.at[pl.ds(i * 256, 256)], sems.at[6 + i])
        copy.start()
        copies.append(copy)
    for copy in copies:
        copy.wait()


def shards(tokens, out_grad, weight_codes, block_scales, proj_basis, first_prev, second_prev):
    any_spec = pl.BlockSpec(memory_space=pl.ANY)
    vmem_spec = pl.BlockSpec(memory_space=pltpu.VMEM)
    held = pl.pallas_call(
        exchange,
        name="exchange",
        out_shape=(
            pltpu.VMEM((TOK, D), BF16),
            pltpu.VMEM((RANK, 1024), BF16),
            pltpu.VMEM((32, 1024), F32),
            pltpu.VMEM((32, 1024), F32),
            pltpu.VMEM((1024, N), BF16),
        ),
        in_specs=[any_spec] * 7,
        out_specs=(vmem_spec,) * 5,
        scratch_shapes=[
            pltpu.VMEM((8, 512, 1024), BF16),
            pltpu.VMEM((2, 512, 1024), BF16),
            pltpu.VMEM((8, 2, 512, 256), BF16),
            pltpu.VMEM((1024, 1024), BF16),
            pltpu.VMEM((8, 1024), F32),
            pltpu.VMEM((1024, 512), BF16),
            pltpu.VMEM((4, 512, 1024), BF16),
            pltpu.VMEM((512, 512), BF16),
            pltpu.VMEM((8, 256, 1024), BF16),
            pltpu.VMEM((8, 256, 1024), BF16),
            pltpu.VMEM((LAG + 1, 256, 1024), F32),
            pltpu.VMEM((8, 256, 1024), BF16),
            pltpu.VMEM((8, 64, 1024), BF16),
            pltpu.VMEM((8, 64, 1024), BF16),
            pltpu.VMEM((8, 2, 64, 1024), BF16),
            pltpu.VMEM((4, 2, 64, 1024), BF16),
            pltpu.VMEM((4, 3, 32, 1024), BF16),
            pltpu.VMEM((3, 32, 1024), BF16),
            pltpu.VMEM((3, 32, 1024), BF16),
            pltpu.VMEM((32, 1024), F32),
            pltpu.VMEM((32, 1024), F32),
            pltpu.SemaphoreType.DMA((COPIES,)),
            pltpu.SemaphoreType.DMA((COPIES,)),
            pltpu.SemaphoreType.DMA((16,)),
        ],
        compiler_params=pltpu.CompilerParams(
            collective_id=0, has_side_effects=True, vmem_limit_bytes=50 * 2**20
        ),
        cost_estimate=pl.CostEstimate(flops=14 * 10**9, bytes_accessed=13 * 2**20, transcendentals=0),
    )(tokens, out_grad, weight_codes, block_scales.T, proj_basis, first_prev.T, second_prev.T)
    ig, first, second, weight = pl.pallas_call(
        write_out,
        name="write_out",
        out_shape=(
            jax.ShapeDtypeStruct((TOK, D), BF16),
            jax.ShapeDtypeStruct((32, 1024), F32),
            jax.ShapeDtypeStruct((32, 1024), F32),
            jax.ShapeDtypeStruct((1024, N), BF16),
        ),
        in_specs=[vmem_spec] * 6,
        out_specs=(any_spec,) * 4,
        scratch_shapes=[pltpu.VMEM((1024, 1024), BF16), pltpu.SemaphoreType.DMA((10,))],
        compiler_params=pltpu.CompilerParams(vmem_limit_bytes=16 * 2**20),
        cost_estimate=pl.CostEstimate(flops=10**9, bytes_accessed=14 * 2**20, transcendentals=0),
    )(*held, proj_basis)
    return ig, first.T, second.T, weight


def solution(mesh):
    in_specs = (
        P(("dp", "fsdp"), None),
        P(("dp", "fsdp"), None),
        P("fsdp", None),
        P("fsdp", None),
        P(),
        P("fsdp", "dp"),
        P("fsdp", "dp"),
    )
    out_specs = (P(("dp", "fsdp"), None), P("fsdp", "dp"), P("fsdp", "dp"), P("fsdp", None))
    return jax.shard_map(shards, mesh=mesh, in_specs=in_specs, out_specs=out_specs, check_vma=False)
```

```python
import math

import jax
import jax.numpy as jnp
from jax import lax
from jax.experimental import pallas as pl
from jax.experimental.pallas import tpu as pltpu
from jax.sharding import PartitionSpec as P

MESH = pl.DeviceIdType.MESH
BF16 = jnp.bfloat16
F32 = jnp.float32
beta_one = 0.9
beta_two = 0.999
learn_rate = 0.2
epsilon = 1e-08

D = 8192
N = 1024
RANK = 512
TOK = 512
OWN = 3
CHUNKS = ((1, 0, 1024), (2, 0, 1024), (3, 0, 1024), (0, 0, 512), (0, 512, 512))
OWN_AT = 3
ORDER = (
    ("P", 0), ("W0b",), ("P", 1), ("P", 2), ("M", 0, 0, 1), ("C", 0), ("E", 0), ("P", 3), ("C", 1), ("P", 4),
    ("C", 2), ("E", 1), ("E", 2), ("Fxc0", 0), ("P", 5), ("M", 0, 0, 0), ("C", 3), ("P", 6), ("C", 4), ("P", 7),
    ("Fxc0", 3), ("E", 3), ("E", 4), ("D2",), ("R", 0), ("C", 5), ("P", 8), ("C", 6), ("C", 7), ("E", 6), ("E", 7),
    ("E", 5), ("P", 9), ("Fxc0", 1), ("R", 2), ("R", 1), ("C", 8), ("E", 8), ("Fzp", 1), ("M", 3, 0, 0), ("C", 9),
    ("E", 9), ("M", 1, 0, 1), ("Fxc0", 2), ("Fzm", 2), ("M", 0, 1, 0), ("Fxc3", 1), ("R", 4), ("R", 3), ("Fzm", 1),
    ("Fzp", 0), ("Fzp", 2), ("M", 0, 1, 1), ("Fxc1", 2), ("Y", 0), ("R", 5), ("Fzm", 3), ("Fzp", 3), ("M", 3, 0, 1),
    ("R", 7), ("Fxc1", 1), ("R", 6), ("M", 1, 0, 0), ("Fxc3", 2), ("Fo1", 3), ("Y", 1), ("F2", 1), ("Y", 2), ("R", 9),
    ("R", 8), ("Fxc3", 3), ("X", 0), ("Y", 3), ("M", 2, 0, 1), ("M", 2, 0, 0), ("Fo3", 0), ("Y", 4), ("Y", 5),
    ("M", 3, 1, 1), ("Y", 7), ("Y", 6), ("X", 1), ("Y", 8), ("Y", 9), ("Fzm", 0), ("M", 1, 1, 1), ("X", 2), ("F2", 2),
    ("Fxc2", 1), ("X", 3), ("Fr3", 0), ("M", 3, 1, 0), ("Fr1", 3), ("X", 4), ("U", 1), ("U", 0), ("Fxc1", 0),
    ("T", 1), ("T", 0), ("Fxc2", 2), ("M", 2, 1, 0), ("S", 1), ("M", 1, 1, 0), ("S", 0), ("M", 2, 1, 1),
)
NT = (((1,), (1,)), ((), ()))


class Net:
    def __init__(self, send_sems, recv_sems, rows):
        self.send_sems, self.recv_sems, self.rows = send_sems, recv_sems, rows
        self.sems, self.got, self.sent = {}, set(), [0]

    def start(self, name, src, dst, device):
        size = math.prod(dst.shape) // N
        if self.sent[-1] + size > self.rows.shape[0]:
            self.sent.append(0)
        self.sent[-1] += size
        at, copies = self.sems.setdefault(name, (len(self.sems), []))
        copy = pltpu.make_async_remote_copy(
            src_ref=src,
            dst_ref=dst,
            send_sem=self.send_sems.at[len(self.sent) - 1],
            recv_sem=self.recv_sems.at[at],
            device_id=device,
            device_id_type=MESH,
        )
        copy.start()
        copies.append(size)

    def recv(self, name):
        if name not in self.got:
            self.got.add(name)
            at, copies = self.sems[name]
            whole = self.rows.at[: sum(copies)]
            pltpu.make_async_copy(whole, whole, self.recv_sems.at[at]).wait()

    def finish(self):
        for name in self.sems:
            self.recv(name)
        for at, size in enumerate(self.sent):
            whole = self.rows.at[:size]
            pltpu.make_async_copy(whole, whole, self.send_sems.at[at]).wait()


RECV_SEMS = 90
SEND_SEMS = 3


def exchange(
    tokens, out_grad, codes, scales, basis, first_prev, second_prev,
    ig, step_all, first_new, second_new, weight,
    W, og, stage, cod, sca, bas, tok, proj_t, sib_out, sib_in, own, cs, rr, s2, y_in, cs2, x_in, low, z_out, z_in,
    fp, sp, send_sems, recv_sems, load_sems,
):
    d = lax.axis_index("dp")
    f = lax.axis_index("fsdp")
    xlo, y, c = d // 8, (d // 2) % 4, d % 2
    z, xhi = f // 2, f % 2

    def dev(dx=0, dh=0, dy=0, dz=0, dc=0):
        xl = 1 - xlo if dx else xlo
        xh = 1 - xhi if dh else xhi
        cc = 1 - c if dc else c
        return (xl * 8 + ((y + dy) % 4) * 2 + cc, ((z + dz) % 4) * 2 + xh)

    sib = dev(dc=1)
    zp, zm = dev(dz=1), dev(dz=3)
    yp, ym = dev(dy=1), dev(dy=3)
    xc, xs, xo = dev(dx=1, dh=1), dev(dx=1), dev(dh=1)
    peers = [sib, zp, zm, dev(dz=2), xc, xs, xo] + [dev(dx=j // 4, dy=j % 4) for j in (1, 2, 3, 5, 6, 7)]

    loads = {}

    def load(name, src, dst):
        copy = pltpu.make_async_copy(src, dst, load_sems.at[len(loads)])
        loads[name] = copy
        copy.start()

    half = pl.multiple_of(c * 512, 512)
    other = pl.multiple_of(512 - c * 512, 512)
    load("scales", scales, sca)
    load("own_codes", codes.at[pl.ds(half, 512)], cod.at[pl.ds(half, 512)])
    load("og", out_grad, og.at[0])
    load("basis", basis, bas)

    def part(q):
        dz, at, width = CHUNKS[q // 2]
        h = 1 - q % 2
        return dz, h, ((dz + 3) % 4) * 2 + h, slice(at, at + width), width

    def load_tokens(q):
        dz, h, _, cols, width = part(q)
        at = (((z + dz) % 4) * 2 + (1 - xhi if h else xhi)) * 1024 + cols.start
        src = tokens.at[:, pl.ds(pl.multiple_of(at, 512), width)]
        load(("tok", q), src, tok.at[q % 4, :, :width])

    for q in range(4):
        load_tokens(q)
    load("other_codes", codes.at[pl.ds(other, 512)], cod.at[pl.ds(other, 512)])
    load("fp", first_prev, fp)
    load("sp", second_prev, sp)

    barrier = pltpu.get_barrier_semaphore()
    for peer in peers:
        pl.semaphore_signal(barrier, inc=1, device_id=peer, device_id_type=MESH)

    def dequantize(base, tiles, also):
        for i in tiles:
            rows = pl.ds(pl.multiple_of(base + i * 128, 128), 128)
            s = jnp.transpose(sca[:, rows])
            for g in range(8):
                cols = slice(g * 128, (g + 1) * 128)
                w = (cod[rows, cols].astype(F32) * s[:, g : g + 1]).astype(BF16)
                weight[rows, cols] = w
                if also:
                    W[i * 128 : (i + 1) * 128, cols] = w

    loads["scales"].wait()
    loads["own_codes"].wait()
    dequantize(half, (0, 3), True)
    pl.semaphore_wait(barrier, len(peers))
    net = Net(send_sems, recv_sems, W)

    def half_of(i, xl):
        return i * 128 + xl * 64

    def wsend(name, way, dz, h, start, size):
        device, to_dz, to_h = {
            "z+": (zp, (dz + 3) % 4, h),
            "z-": (zm, (dz + 1) % 4, h),
            "xc": (xc, dz, 1 - h),
            "xs": (xs, dz, h),
        }[way]
        src, dst = ((dz * 2 + h) * 512 + start, (to_dz * 2 + to_h) * 512 + start)
        if not isinstance(start, int):
            src, dst = pl.multiple_of(src, 32), pl.multiple_of(dst, 32)
        net.start(name, W.at[pl.ds(src, size)], W.at[pl.ds(dst, size)], device)

    wsend(("zp", 0), "z+", 0, 0, 0, 128)
    wsend(("zm", 3), "z-", 0, 0, 384, 128)
    wsend(("xc0", 0), "xc", 0, 0, half_of(0, xlo), 64)
    wsend(("xc0", 3), "xc", 0, 0, half_of(3, xlo), 64)

    loads["og"].wait()
    loads["basis"].wait()
    projected = jnp.dot(og[0], bas[...], preferred_element_type=F32).astype(BF16)
    turned = jnp.transpose(projected)
    for j in range(16):
        jx, jy, jc = j // 8, (j // 2) % 4, j % 2
        row = jnp.where(c == jc, 0, 256) + ((jy - y + 4) % 4) * 64 + jx * 32
        proj_t[pl.ds(pl.multiple_of(row, 32), 32), :] = turned[j * 32 : (j + 1) * 32, :]

    def multiply(q):
        _, _, slot, span, width = part(q)
        loads["tok", q].wait()

        for i in range(0, width, 256):
            acc = jnp.dot(proj_t[...], tok[q % 4, :, i : i + 256], preferred_element_type=F32)
            own[q % OWN, :, i : i + 256] = acc[:256]
            sib_out[slot, :, span.start + i : span.start + i + 256] = acc[256:].astype(BF16)
        if q + 4 < 2 * len(CHUNKS):
            load_tokens(q + 4)

    def P(q):
        _, _, slot, cols, _ = part(q)
        multiply(q)
        if q == 0:
            net.start(("og",), og.at[0], og.at[1], sib)
        net.start(("sib", q), sib_out.at[slot, :, cols], sib_in.at[slot, :, cols], sib)

    def C(q):
        _, h, slot, cols, width = part(q)
        net.recv(("sib", q))

        def tile(i, carry):
            rows = pl.ds(pl.multiple_of(i * 64, 64), 64)
            total = own[q % OWN, rows, :width] + sib_in[slot, rows, cols].astype(F32)
            cs[slot, rows, cols] = total.astype(BF16)
            return carry

        lax.fori_loop(0, 4, tile, 0)
        net.start(("far", q), cs.at[slot, 128:192, cols], rr.at[slot, :, cols], yp if h else ym)

    def E(q):
        _, h, slot, cols, _ = part(q)
        rows = slice(192, 256) if h else slice(64, 128)
        net.start(("y", q), cs.at[slot, rows, cols], y_in.at[slot, h, :, cols], ym if h else yp)

    def R(q):
        _, h, slot, cols, _ = part(q)
        net.recv(("far", q))
        rows = slice(64, 128) if h else slice(192, 256)
        s2[slot, :, cols] = (cs[slot, rows, cols].astype(F32) + rr[slot, :, cols].astype(F32)).astype(BF16)
        net.start(("y", q), s2.at[slot, :, cols], y_in.at[slot, 1 - h, :, cols], yp if h else ym)

    def Y(q):
        _, h, slot, cols, _ = part(q)
        net.recv(("y", q))
        total = cs[slot, 0:64, cols].astype(F32) + y_in[slot, 0, :, cols].astype(F32)
        cs2[slot, :, cols] = (total + y_in[slot, 1, :, cols].astype(F32)).astype(BF16)
        for n, to, xl in ((0, xc, 1 - xlo), (2, xo, xlo)) if h else ((1, xs, 1 - xlo),):
            rows = pl.ds(pl.multiple_of(xl * 32, 32), 32)
            net.start(("x", q // 2), cs2.at[slot, rows, cols], x_in.at[slot // 2, n, :, cols], to)

    def X(k):
        dz, _, slot, cols, _ = part(2 * k + 1)
        total = cs2[slot, pl.ds(pl.multiple_of(xlo * 32, 32), 32), cols].astype(F32)
        net.recv(("x", k))
        for n in range(3):
            total = total + x_in[slot // 2, n, :, cols].astype(F32)
        if dz == 0:
            low[:, cols] = total
        else:
            z_out[dz - 1] = total.astype(BF16)
            net.start(("z",), z_out.at[dz - 1], z_in.at[dz - 1], dev(dz=dz))

    def U(j):
        cols = part(2 * OWN_AT + 2 * j)[3]
        total = low[:, cols]
        net.recv(("z",))
        for dz in (1, 2, 3):
            total = total + z_in[dz - 1, :, cols].astype(F32)
        for name in ("fp", "sp"):
            if name in loads:
                loads.pop(name).wait()
        first = beta_one * fp[:, cols] + (1.0 - beta_one) * total
        second = beta_two * sp[:, cols] + (1.0 - beta_two) * total * total
        first_new[:, cols] = first
        second_new[:, cols] = second
        step_all[xlo * 4 + y, c, :, cols] = (first / (jnp.sqrt(second) + epsilon)).astype(BF16)
        mine = step_all.at[xlo * 4 + y, c, :, cols]
        net.start(("sx", j), mine, mine, xs)
        for i in (1, 3, 2):
            net.start(("step", j), mine, mine, dev(dy=i))

    def T(j):
        cols = part(2 * OWN_AT + 2 * j)[3]
        net.recv(("sx", j))
        theirs = step_all.at[(1 - xlo) * 4 + y, c, :, cols]
        for i in (1, 3, 2):
            net.start(("step", j), theirs, theirs, dev(dy=i))

    def S(j):
        cols = part(2 * OWN_AT + 2 * j)[3]
        net.recv(("step", j))
        ours = step_all.at[:, c, :, cols]
        net.start(("ss",), ours, ours, sib)

    def D2():
        loads["other_codes"].wait()
        dequantize(other, range(4), False)

    def Fzp(i):
        net.recv(("zp", i))
        if i < 2:
            wsend(("zpp", i), "z+", 3, 0, i * 128, 128)
        if i != 0:
            wsend(("xc3", i), "xc", 3, 0, half_of(i, xlo), 64)

    def Fzm(i):
        net.recv(("zm", i))
        if i >= 2:
            wsend(("zmm", i), "z-", 1, 0, i * 128, 128)
        if i != 3:
            wsend(("xc1", i), "xc", 1, 0, half_of(i, xlo), 64)

    def forward_x(dz):
        def run(i):
            net.recv(("xc%d" % dz, i))
            wsend(("xs%d" % dz, i), "xs", dz, 1, half_of(i, 1 - xlo), 64)

        return run

    def Fo3(i):
        net.recv(("xc0", i))
        net.recv(("xs0", i))
        wsend(("zo3", i), "z+", 0, 1, i * 128, 128)

    def Fo1(i):
        net.recv(("xc0", i))
        net.recv(("xs0", i))
        wsend(("zo1", i), "z-", 0, 1, i * 128, 128)

    def Fr3(i):
        net.recv(("zo3", i))
        wsend(("zr3", i), "z+", 3, 1, i * 128, 128)

    def Fr1(i):
        net.recv(("zo1", i))
        wsend(("zr1", i), "z-", 1, 1, i * 128, 128)

    def F2(i):
        net.recv(("zpp", i) if i < 2 else ("zmm", i))
        wsend(("xc2", i), "xc", 2, 0, half_of(i, xlo), 64)

    def M(dz, h, u):
        for i in (2 * u, 2 * u + 1):
            if h == 0:
                if dz:
                    net.recv((None, "zm", "zpp" if i < 2 else "zmm", "zp")[dz : dz + 1] + (i,))
            elif (dz, i) in ((3, 0), (1, 3)):
                net.recv(("zo%d" % dz, i))
            elif dz == 2 and i in (0, 3):
                net.recv(("zr%d" % (1 if i else 3), i))
            else:
                net.recv(("xc%d" % dz, i))
                net.recv(("xs%d" % dz, i))
        net.recv(("og",))
        slot = dz * 2 + h
        fsdp = ((z + dz) % 4) * 2 + (1 - xhi if h else xhi)
        cols = pl.ds(pl.multiple_of(fsdp * 1024 + c * 512 + u * 256, 256), 256)

        at = slot * 512 + u * 256

        def tile(i, carry):
            rows = pl.ds(pl.multiple_of(i * 256, 256), 256)
            w = W[at : at + 256, :]
            theirs = lax.dot_general(og[1, rows, :], w, NT, preferred_element_type=F32)
            stage[slot, u, rows, :] = theirs.astype(BF16)
            mine = lax.dot_general(og[0, rows, :], w, NT, preferred_element_type=F32)
            ig[rows, cols] = mine.astype(BF16)
            return carry

        lax.fori_loop(0, 2, tile, 0)
        net.start(("ig",), stage.at[slot, u], ig.at[:, cols], sib)

    def W0b():
        dequantize(half, (1, 2), True)
        wsend(("zp", 1), "z+", 0, 0, 128, 128)
        wsend(("zm", 2), "z-", 0, 0, 256, 128)
        wsend(("xc0", 1), "xc", 0, 0, half_of(1, xlo), 64)
        wsend(("xc0", 2), "xc", 0, 0, half_of(2, xlo), 64)
        wsend(("zp", 2), "z+", 0, 0, 256, 128)
        wsend(("zm", 1), "z-", 0, 0, 128, 128)
        wsend(("zp", 3), "z+", 0, 0, 384, 128)
        wsend(("zm", 0), "z-", 0, 0, 0, 128)

    steps = dict(
        W0b=W0b,
        P=P, C=C, E=E, R=R, Y=Y, X=X, U=U, T=T, S=S, M=M, D2=D2, Fzp=Fzp, Fzm=Fzm, Fo3=Fo3, Fo1=Fo1, Fr3=Fr3,
        Fr1=Fr1, F2=F2, Fxc0=forward_x(0), Fxc1=forward_x(1), Fxc2=forward_x(2), Fxc3=forward_x(3),
    )
    for name, *place in ORDER:
        steps[name](*place)
    net.finish()


def write_out(ig, step_all, first_new, second_new, weight, basis, ig_out, first_out, second_out, weight_out, nw, sems):
    copies = [
        pltpu.make_async_copy(ig.at[pl.ds(i * 128, 128)], ig_out.at[pl.ds(i * 128, 128)], sems.at[i]) for i in range(4)
    ]
    copies.append(pltpu.make_async_copy(first_new, first_out, sems.at[4]))
    copies.append(pltpu.make_async_copy(second_new, second_out, sems.at[5]))
    for copy in copies:
        copy.start()
    for i in range(4):
        rows = slice(i * 256, (i + 1) * 256)
        step = jnp.transpose(step_all[:, :, :, rows].reshape(RANK, 256))
        change = lax.dot_general(step, basis[...], NT, preferred_element_type=F32)
        nw[rows, :] = (weight[rows, :].astype(F32) - learn_rate * change).astype(BF16)
        copy = pltpu.make_async_copy(nw.at[pl.ds(i * 256, 256)], weight_out.at[pl.ds(i * 256, 256)], sems.at[6 + i])
        copy.start()
        copies.append(copy)
    for copy in copies:
        copy.wait()


def shards(tokens, out_grad, weight_codes, block_scales, proj_basis, first_prev, second_prev):
    any_spec = pl.BlockSpec(memory_space=pl.ANY)
    vmem_spec = pl.BlockSpec(memory_space=pltpu.VMEM)
    held = pl.pallas_call(
        exchange,
        name="exchange",
        out_shape=(
            pltpu.VMEM((TOK, D), BF16),
            pltpu.VMEM((8, 2, 32, 1024), BF16),
            pltpu.VMEM((32, 1024), F32),
            pltpu.VMEM((32, 1024), F32),
            pltpu.VMEM((1024, N), BF16),
        ),
        in_specs=[any_spec] * 7,
        out_specs=(vmem_spec,) * 5,
        scratch_shapes=[
            pltpu.VMEM((4096, 1024), BF16),
            pltpu.VMEM((2, 512, 1024), BF16),
            pltpu.VMEM((8, 2, 512, 256), BF16),
            pltpu.VMEM((1024, 1024), BF16),
            pltpu.VMEM((8, 1024), F32),
            pltpu.VMEM((1024, 512), BF16),
            pltpu.VMEM((4, 512, 1024), BF16),
            pltpu.VMEM((512, 512), BF16),
            pltpu.VMEM((8, 256, 1024), BF16),
            pltpu.VMEM((8, 256, 1024), BF16),
            pltpu.VMEM((OWN, 256, 1024), F32),
            pltpu.VMEM((8, 256, 1024), BF16),
            pltpu.VMEM((8, 64, 1024), BF16),
            pltpu.VMEM((8, 64, 1024), BF16),
            pltpu.VMEM((8, 2, 64, 1024), BF16),
            pltpu.VMEM((8, 64, 1024), BF16),
            pltpu.VMEM((4, 3, 32, 1024), BF16),
            pltpu.VMEM((32, 1024), F32),
            pltpu.VMEM((3, 32, 1024), BF16),
            pltpu.VMEM((3, 32, 1024), BF16),
            pltpu.VMEM((32, 1024), F32),
            pltpu.VMEM((32, 1024), F32),
            pltpu.SemaphoreType.DMA((SEND_SEMS,)),
            pltpu.SemaphoreType.DMA((RECV_SEMS,)),
            pltpu.SemaphoreType.DMA((17,)),
        ],
        compiler_params=pltpu.CompilerParams(
            collective_id=0, has_side_effects=True, vmem_limit_bytes=50 * 2**20
        ),
        cost_estimate=pl.CostEstimate(flops=14 * 10**9, bytes_accessed=13 * 2**20, transcendentals=0),
    )(tokens, out_grad, weight_codes, block_scales.T, proj_basis, first_prev.T, second_prev.T)
    ig, first, second, weight = pl.pallas_call(
        write_out,
        name="write_out",
        out_shape=(
            jax.ShapeDtypeStruct((TOK, D), BF16),
            jax.ShapeDtypeStruct((32, 1024), F32),
            jax.ShapeDtypeStruct((32, 1024), F32),
            jax.ShapeDtypeStruct((1024, N), BF16),
        ),
        in_specs=[vmem_spec] * 6,
        out_specs=(any_spec,) * 4,
        scratch_shapes=[pltpu.VMEM((1024, 1024), BF16), pltpu.SemaphoreType.DMA((10,))],
        compiler_params=pltpu.CompilerParams(vmem_limit_bytes=16 * 2**20),
        cost_estimate=pl.CostEstimate(flops=10**9, bytes_accessed=14 * 2**20, transcendentals=0),
    )(*held, proj_basis)
    return ig, first.T, second.T, weight


def solution(mesh):
    in_specs = (
        P(("dp", "fsdp"), None),
        P(("dp", "fsdp"), None),
        P("fsdp", None),
        P("fsdp", None),
        P(),
        P("fsdp", "dp"),
        P("fsdp", "dp"),
    )
    out_specs = (P(("dp", "fsdp"), None), P("fsdp", "dp"), P("fsdp", "dp"), P("fsdp", None))
    return jax.shard_map(shards, mesh=mesh, in_specs=in_specs, out_specs=out_specs, check_vma=False)
```

```python
import math

import jax
import jax.numpy as jnp
from jax import lax
from jax.experimental import pallas as pl
from jax.experimental.pallas import tpu as pltpu
from jax.sharding import PartitionSpec as P

MESH = pl.DeviceIdType.MESH
BF16 = jnp.bfloat16
F32 = jnp.float32
beta_one = 0.9
beta_two = 0.999
learn_rate = 0.2
epsilon = 1e-08

D = 8192
N = 1024
RANK = 512
TOK = 512
OWN = 3
CHUNKS = ((1, 0, 1024), (2, 0, 1024), (3, 0, 1024), (0, 0, 512), (0, 512, 512))
OWN_AT = 3
ORDER = (
    ("P", 0), ("W0b",), ("P", 1), ("P", 2), ("C", 0), ("C", 1), ("C", 2), ("E", 0), ("P", 3), ("Fxc0", 0), ("P", 4),
    ("M", 0, 0, 0), ("Fxc0", 3), ("C", 3), ("P", 5), ("P", 6), ("Fxc0", 1), ("E", 2), ("C", 4), ("M", 0, 0, 1),
    ("R", 0), ("C", 5), ("Fzm", 2), ("E", 1), ("E", 3), ("P", 7), ("Fxc0", 2), ("Fzp", 1), ("Fxc1", 2), ("R", 1),
    ("Fzm", 1), ("R", 3), ("P", 8), ("Y", 0), ("M", 3, 0, 0), ("C", 6), ("E", 5), ("M", 0, 1, 0), ("R", 5), ("C", 8),
    ("P", 9), ("R", 2), ("Fxc3", 1), ("Fzm", 0), ("Fo3", 0), ("Fxc1", 1), ("Fo1", 3), ("M", 1, 0, 1), ("R", 4),
    ("C", 7), ("Fzp", 3), ("Y", 1), ("R", 6), ("E", 4), ("Y", 3), ("M", 1, 0, 0), ("F2", 1), ("Fzp", 0),
    ("M", 0, 1, 1), ("Fxc1", 0), ("E", 6), ("F2", 2), ("Y", 5), ("C", 9), ("D2",), ("Y", 2), ("R", 8), ("R", 7),
    ("Fr3", 0), ("Fxc2", 1), ("Fr1", 3), ("E", 7), ("X", 0), ("E", 9), ("Y", 4), ("E", 8), ("Fxc2", 2),
    ("M", 3, 1, 0), ("R", 9), ("X", 1), ("Y", 6), ("Y", 7), ("Y", 8), ("Fyw", 1), ("Fyw", 3), ("X", 2), ("Fzm", 3),
    ("Y", 9), ("Fxc3", 3), ("Fzp", 2), ("M", 1, 1, 0), ("Fyw", 2), ("Fyw", 0), ("M", 3, 0, 1), ("X", 3), ("U", 0),
    ("X", 4), ("U", 1), ("M", 2, 0, 0), ("Fxc3", 2), ("M", 1, 1, 1), ("T", 0), ("M", 2, 1, 1), ("T", 1),
    ("M", 2, 0, 1), ("M", 2, 1, 0), ("M", 3, 1, 1), ("S", 0), ("S", 1),
)
NT = (((1,), (1,)), ((), ()))
TN = (((0,), (1,)), ((), ()))


class Net:
    def __init__(self, send_sems, recv_sems, rows):
        self.send_sems, self.recv_sems, self.rows = send_sems, recv_sems, rows
        self.sems, self.got, self.sent = {}, set(), [0]

    def start(self, name, src, dst, device):
        size = math.prod(dst.shape) // N
        if self.sent[-1] + size > self.rows.shape[0]:
            self.sent.append(0)
        self.sent[-1] += size
        at, copies = self.sems.setdefault(name, (len(self.sems), []))
        copy = pltpu.make_async_remote_copy(
            src_ref=src,
            dst_ref=dst,
            send_sem=self.send_sems.at[len(self.sent) - 1],
            recv_sem=self.recv_sems.at[at],
            device_id=device,
            device_id_type=MESH,
        )
        copy.start()
        copies.append(size)

    def recv(self, name):
        if name not in self.got:
            self.got.add(name)
            at, copies = self.sems[name]
            whole = self.rows.at[: sum(copies)]
            pltpu.make_async_copy(whole, whole, self.recv_sems.at[at]).wait()

    def finish(self):
        for name in self.sems:
            self.recv(name)
        for at, size in enumerate(self.sent):
            whole = self.rows.at[:size]
            pltpu.make_async_copy(whole, whole, self.send_sems.at[at]).wait()


RECV_SEMS = 88
SEND_SEMS = 3


def update_rows(rows, step_all, basis, weight, out):
    step = step_all[:, :, :, rows].reshape(RANK, 512)
    change = lax.dot_general(step, basis[...], TN, preferred_element_type=F32)
    out[0:512, :] = (weight[rows, :].astype(F32) - learn_rate * change).astype(BF16)


def exchange(
    tokens, out_grad, codes, scales, basis, first_prev, second_prev,
    ig, step_all, first_new, second_new, weight,
    W, og, stage, cod, sca, bas, tok, proj_t, sib_out, sib_in, own, cs, rr, s2, y_in, cs2, x_in, low, z_out, z_in,
    fp, sp, send_sems, recv_sems, load_sems,
):
    d = lax.axis_index("dp")
    f = lax.axis_index("fsdp")
    xlo, y, c = d // 8, (d // 2) % 4, d % 2
    z, xhi = f // 2, f % 2

    def dev(dx=0, dh=0, dy=0, dz=0, dc=0):
        xl = 1 - xlo if dx else xlo
        xh = 1 - xhi if dh else xhi
        cc = 1 - c if dc else c
        return (xl * 8 + ((y + dy) % 4) * 2 + cc, ((z + dz) % 4) * 2 + xh)

    sib = dev(dc=1)
    zp, zm = dev(dz=1), dev(dz=3)
    yp, ym = dev(dy=1), dev(dy=3)
    xc, xs, xo = dev(dx=1, dh=1), dev(dx=1), dev(dh=1)
    peers = [sib, zp, zm, dev(dz=2), xc, xs, xo] + [dev(dx=j // 4, dy=j % 4) for j in (1, 2, 3, 5, 6, 7)]

    loads = {}

    def load(name, src, dst):
        copy = pltpu.make_async_copy(src, dst, load_sems.at[len(loads)])
        loads[name] = copy
        copy.start()

    half = pl.multiple_of(c * 512, 512)
    other = pl.multiple_of(512 - c * 512, 512)
    load("scales", scales, sca)
    load("own_codes", codes.at[pl.ds(half, 512)], cod.at[pl.ds(half, 512)])
    load("og", out_grad, og.at[0])
    load("basis", basis, bas)

    def part(q):
        dz, at, width = CHUNKS[q // 2]
        h = 1 - q % 2
        return dz, h, ((dz + 3) % 4) * 2 + h, slice(at, at + width), width

    def load_tokens(q):
        dz, h, _, cols, width = part(q)
        at = (((z + dz) % 4) * 2 + (1 - xhi if h else xhi)) * 1024 + cols.start
        src = tokens.at[:, pl.ds(pl.multiple_of(at, 512), width)]
        load(("tok", q), src, tok.at[q % 4, :, :width])

    for q in range(4):
        load_tokens(q)
    load("other_codes", codes.at[pl.ds(other, 512)], cod.at[pl.ds(other, 512)])
    load("fp", first_prev, fp)
    load("sp", second_prev, sp)

    barrier = pltpu.get_barrier_semaphore()
    for peer in peers:
        pl.semaphore_signal(barrier, inc=1, device_id=peer, device_id_type=MESH)

    def dequantize(base, tiles, also):
        for i in tiles:
            rows = pl.ds(pl.multiple_of(base + i * 128, 128), 128)
            s = jnp.transpose(sca[:, rows])
            for g in range(8):
                cols = slice(g * 128, (g + 1) * 128)
                w = (cod[rows, cols].astype(F32) * s[:, g : g + 1]).astype(BF16)
                weight[rows, cols] = w
                if also:
                    W[i * 128 : (i + 1) * 128, cols] = w

    loads["scales"].wait()
    loads["own_codes"].wait()
    dequantize(half, (0, 3), True)
    pl.semaphore_wait(barrier, len(peers))
    net = Net(send_sems, recv_sems, W)

    def half_of(i, xl):
        return i * 128 + xl * 64

    def wsend(name, way, dz, h, start, size):
        device, to_dz, to_h = {
            "z+": (zp, (dz + 3) % 4, h),
            "z-": (zm, (dz + 1) % 4, h),
            "xc": (xc, dz, 1 - h),
            "xs": (xs, dz, h),
            "y+": (yp, dz, h),
            "y-": (ym, dz, h),
        }[way]
        src, dst = ((dz * 2 + h) * 512 + start, (to_dz * 2 + to_h) * 512 + start)
        if not isinstance(start, int):
            src, dst = pl.multiple_of(src, 32), pl.multiple_of(dst, 32)
        net.start(name, W.at[pl.ds(src, size)], W.at[pl.ds(dst, size)], device)

    wsend(("zp", 0), "z+", 0, 0, 0, 128)
    wsend(("zm", 3), "z-", 0, 0, 384, 128)
    wsend(("xc0", 0), "xc", 0, 0, half_of(0, xlo), 64)
    wsend(("xc0", 3), "xc", 0, 0, half_of(3, xlo), 64)

    loads["og"].wait()
    loads["basis"].wait()
    projected = jnp.dot(og[0], bas[...], preferred_element_type=F32).astype(BF16)
    turned = jnp.transpose(projected)
    for j in range(16):
        jx, jy, jc = j // 8, (j // 2) % 4, j % 2
        row = jnp.where(c == jc, 0, 256) + ((jy - y + 4) % 4) * 64 + jx * 32
        proj_t[pl.ds(pl.multiple_of(row, 32), 32), :] = turned[j * 32 : (j + 1) * 32, :]

    def multiply(q):
        _, _, slot, span, width = part(q)
        loads["tok", q].wait()

        for i in range(0, width, 256):
            acc = jnp.dot(proj_t[...], tok[q % 4, :, i : i + 256], preferred_element_type=F32)
            own[q % OWN, :, i : i + 256] = acc[:256]
            sib_out[slot, :, span.start + i : span.start + i + 256] = acc[256:].astype(BF16)
        if q + 4 < 2 * len(CHUNKS):
            load_tokens(q + 4)

    def P(q):
        _, _, slot, cols, _ = part(q)
        multiply(q)
        if q == 0:
            net.start(("og",), og.at[0], og.at[1], sib)
        net.start(("sib", q), sib_out.at[slot, :, cols], sib_in.at[slot, :, cols], sib)

    def C(q):
        _, h, slot, cols, width = part(q)
        net.recv(("sib", q))

        def tile(i, carry):
            rows = pl.ds(pl.multiple_of(i * 64, 64), 64)
            total = own[q % OWN, rows, :width] + sib_in[slot, rows, cols].astype(F32)
            cs[slot, rows, cols] = total.astype(BF16)
            return carry

        lax.fori_loop(0, 4, tile, 0)
        net.start(("far", q), cs.at[slot, 128:192, cols], rr.at[slot, :, cols], yp if h else ym)

    def E(q):
        _, h, slot, cols, _ = part(q)
        rows = slice(192, 256) if h else slice(64, 128)
        net.start(("y", q), cs.at[slot, rows, cols], y_in.at[slot, h, :, cols], ym if h else yp)

    def R(q):
        _, h, slot, cols, _ = part(q)
        net.recv(("far", q))
        rows = slice(64, 128) if h else slice(192, 256)
        s2[slot, :, cols] = (cs[slot, rows, cols].astype(F32) + rr[slot, :, cols].astype(F32)).astype(BF16)
        net.start(("y", q), s2.at[slot, :, cols], y_in.at[slot, 1 - h, :, cols], yp if h else ym)

    def Y(q):
        _, h, slot, cols, _ = part(q)
        net.recv(("y", q))
        total = cs[slot, 0:64, cols].astype(F32) + y_in[slot, 0, :, cols].astype(F32)
        cs2[slot, :, cols] = (total + y_in[slot, 1, :, cols].astype(F32)).astype(BF16)
        for n, to, xl in ((0, xc, 1 - xlo), (2, xo, xlo)) if h else ((1, xs, 1 - xlo),):
            rows = pl.ds(pl.multiple_of(xl * 32, 32), 32)
            net.start(("x", q // 2), cs2.at[slot, rows, cols], x_in.at[slot // 2, n, :, cols], to)

    def X(k):
        dz, _, slot, cols, _ = part(2 * k + 1)
        total = cs2[slot, pl.ds(pl.multiple_of(xlo * 32, 32), 32), cols].astype(F32)
        net.recv(("x", k))
        for n in range(3):
            total = total + x_in[slot // 2, n, :, cols].astype(F32)
        if dz == 0:
            low[:, cols] = total
        else:
            z_out[dz - 1] = total.astype(BF16)
            net.start(("z",), z_out.at[dz - 1], z_in.at[dz - 1], dev(dz=dz))

    def U(j):
        cols = part(2 * OWN_AT + 2 * j)[3]
        total = low[:, cols]
        net.recv(("z",))
        for dz in (1, 2, 3):
            total = total + z_in[dz - 1, :, cols].astype(F32)
        for name in ("fp", "sp"):
            if name in loads:
                loads.pop(name).wait()
        first = beta_one * fp[:, cols] + (1.0 - beta_one) * total
        second = beta_two * sp[:, cols] + (1.0 - beta_two) * total * total
        first_new[:, cols] = first
        second_new[:, cols] = second
        step_all[xlo * 4 + y, c, :, cols] = (first / (jnp.sqrt(second) + epsilon)).astype(BF16)
        mine = step_all.at[xlo * 4 + y, c, :, cols]
        net.start(("sx", j), mine, mine, xs)
        for i in (1, 3, 2):
            net.start(("step", j), mine, mine, dev(dy=i))

    def T(j):
        cols = part(2 * OWN_AT + 2 * j)[3]
        net.recv(("sx", j))
        theirs = step_all.at[(1 - xlo) * 4 + y, c, :, cols]
        for i in (1, 3, 2):
            net.start(("step", j), theirs, theirs, dev(dy=i))

    def S(j):
        cols = part(2 * OWN_AT + 2 * j)[3]
        net.recv(("step", j))
        ours = step_all.at[:, c, :, cols]
        net.start(("ss", j), ours, ours, sib)

    def D2():
        loads["other_codes"].wait()
        dequantize(other, range(4), False)

    def Fzp(i):
        net.recv(("zp", i))
        if i < 2:
            wsend(("zpp", i), "z+", 3, 0, i * 128, 128)
        if i != 0:
            wsend(("xc3", i), "xc", 3, 0, half_of(i, xlo), 64)

    def Fzm(i):
        net.recv(("zm", i))
        if i >= 2:
            wsend(("zmm", i), "z-", 1, 0, i * 128, 128)
        if i != 3:
            wsend(("xc1", i), "xc", 1, 0, half_of(i, xlo), 64)

    def forward_x(dz):
        def run(i):
            net.recv(("xc%d" % dz, i))
            wsend(("xs%d" % dz, i), "xs", dz, 1, half_of(i, 1 - xlo), 64)

        return run

    def Fo3(i):
        net.recv(("xc0", i))
        net.recv(("xs0", i))
        wsend(("zo3", i), "z+", 0, 1, i * 128, 128)

    def Fo1(i):
        net.recv(("xc0", i))
        net.recv(("xs0", i))
        wsend(("zo1", i), "z-", 0, 1, i * 128, 128)

    parity = y % 2

    def Fr3(i):
        net.recv(("zo3", i))
        wsend(("zr3", i), "z+", 3, 1, half_of(i, parity), 64)

    def Fr1(i):
        net.recv(("zo1", i))
        wsend(("zr1", i), "z-", 1, 1, half_of(i, parity), 64)

    def F2(i):
        net.recv(("zpp", i) if i < 2 else ("zmm", i))
        wsend(("xc2", i), "xc", 2, 0, half_of(i, parity) + xlo * 32, 32)

    def Fxc2(i):
        net.recv(("xc2", i))
        wsend(("xs2", i), "xs", 2, 1, half_of(i, parity) + (1 - xlo) * 32, 32)

    def Fyw(i):
        if i in (0, 3):
            net.recv(("zr%d" % (1 if i else 3), i))
        else:
            net.recv(("xc2", i))
            net.recv(("xs2", i))
        wsend(("yw", i), "y+" if i < 2 else "y-", 2, 1, half_of(i, parity), 64)

    def M(dz, h, u):
        for i in (2 * u, 2 * u + 1):
            if h == 0:
                if dz:
                    net.recv((None, "zm", "zpp" if i < 2 else "zmm", "zp")[dz : dz + 1] + (i,))
            elif (dz, i) in ((3, 0), (1, 3)):
                net.recv(("zo%d" % dz, i))
            elif dz == 2 and i in (0, 3):
                net.recv(("zr%d" % (1 if i else 3), i))
            else:
                net.recv(("xc%d" % dz, i))
                net.recv(("xs%d" % dz, i))
            if (dz, h) == (2, 1):
                net.recv(("yw", i))
        net.recv(("og",))
        slot = dz * 2 + h
        fsdp = ((z + dz) % 4) * 2 + (1 - xhi if h else xhi)
        cols = pl.ds(pl.multiple_of(fsdp * 1024 + c * 512 + u * 256, 256), 256)

        at = slot * 512 + u * 256

        def tile(i, carry):
            rows = pl.ds(pl.multiple_of(i * 256, 256), 256)
            w = W[at : at + 256, :]
            theirs = lax.dot_general(og[1, rows, :], w, NT, preferred_element_type=F32)
            stage[slot, u, rows, :] = theirs.astype(BF16)
            mine = lax.dot_general(og[0, rows, :], w, NT, preferred_element_type=F32)
            ig[rows, cols] = mine.astype(BF16)
            return carry

        lax.fori_loop(0, 2, tile, 0)
        net.start(("ig",), stage.at[slot, u], ig.at[:, cols], sib)

    def W0b():
        dequantize(half, (1, 2), True)
        wsend(("zp", 1), "z+", 0, 0, 128, 128)
        wsend(("zm", 2), "z-", 0, 0, 256, 128)
        wsend(("xc0", 1), "xc", 0, 0, half_of(1, xlo), 64)
        wsend(("xc0", 2), "xc", 0, 0, half_of(2, xlo), 64)
        wsend(("zp", 2), "z+", 0, 0, 256, 128)
        wsend(("zm", 1), "z-", 0, 0, 128, 128)
        wsend(("zp", 3), "z+", 0, 0, 384, 128)
        wsend(("zm", 0), "z-", 0, 0, 0, 128)

    steps = dict(
        W0b=W0b, Fyw=Fyw,
        P=P, C=C, E=E, R=R, Y=Y, X=X, U=U, T=T, S=S, M=M, D2=D2, Fzp=Fzp, Fzm=Fzm, Fo3=Fo3, Fo1=Fo1, Fr3=Fr3,
        Fr1=Fr1, F2=F2, Fxc0=forward_x(0), Fxc1=forward_x(1), Fxc2=Fxc2, Fxc3=forward_x(3),
    )
    for name, *place in ORDER:
        steps[name](*place)

    net.recv(("ss", 0))
    update_rows(slice(0, 512), step_all, bas, weight, weight)
    net.finish()


def write_out(ig, step_all, first_new, second_new, weight, basis, ig_out, first_out, second_out, weight_out, nw, sems):
    copies = [
        pltpu.make_async_copy(ig.at[pl.ds(i * 128, 128)], ig_out.at[pl.ds(i * 128, 128)], sems.at[i]) for i in range(4)
    ]
    copies.append(pltpu.make_async_copy(first_new, first_out, sems.at[4]))
    copies.append(pltpu.make_async_copy(second_new, second_out, sems.at[5]))
    copies.append(pltpu.make_async_copy(weight.at[pl.ds(0, 512)], weight_out.at[pl.ds(0, 512)], sems.at[6]))
    for copy in copies:
        copy.start()
    update_rows(slice(512, 1024), step_all, basis, weight, nw)
    copy = pltpu.make_async_copy(nw, weight_out.at[pl.ds(512, 512)], sems.at[7])
    copy.start()
    copies.append(copy)
    for copy in copies:
        copy.wait()


def shards(tokens, out_grad, weight_codes, block_scales, proj_basis, first_prev, second_prev):
    any_spec = pl.BlockSpec(memory_space=pl.ANY)
    vmem_spec = pl.BlockSpec(memory_space=pltpu.VMEM)
    held = pl.pallas_call(
        exchange,
        name="exchange",
        out_shape=(
            pltpu.VMEM((TOK, D), BF16),
            pltpu.VMEM((8, 2, 32, 1024), BF16),
            pltpu.VMEM((32, 1024), F32),
            pltpu.VMEM((32, 1024), F32),
            pltpu.VMEM((1024, N), BF16),
        ),
        in_specs=[any_spec] * 7,
        out_specs=(vmem_spec,) * 5,
        scratch_shapes=[
            pltpu.VMEM((4096, 1024), BF16),
            pltpu.VMEM((2, 512, 1024), BF16),
            pltpu.VMEM((8, 2, 512, 256), BF16),
            pltpu.VMEM((1024, 1024), BF16),
            pltpu.VMEM((8, 1024), F32),
            pltpu.VMEM((1024, 512), BF16),
            pltpu.VMEM((4, 512, 1024), BF16),
            pltpu.VMEM((512, 512), BF16),
            pltpu.VMEM((8, 256, 1024), BF16),
            pltpu.VMEM((8, 256, 1024), BF16),
            pltpu.VMEM((OWN, 256, 1024), F32),
            pltpu.VMEM((8, 256, 1024), BF16),
            pltpu.VMEM((8, 64, 1024), BF16),
            pltpu.VMEM((8, 64, 1024), BF16),
            pltpu.VMEM((8, 2, 64, 1024), BF16),
            pltpu.VMEM((8, 64, 1024), BF16),
            pltpu.VMEM((4, 3, 32, 1024), BF16),
            pltpu.VMEM((32, 1024), F32),
            pltpu.VMEM((3, 32, 1024), BF16),
            pltpu.VMEM((3, 32, 1024), BF16),
            pltpu.VMEM((32, 1024), F32),
            pltpu.VMEM((32, 1024), F32),
            pltpu.SemaphoreType.DMA((SEND_SEMS,)),
            pltpu.SemaphoreType.DMA((RECV_SEMS,)),
            pltpu.SemaphoreType.DMA((17,)),
        ],
        compiler_params=pltpu.CompilerParams(
            collective_id=0, has_side_effects=True, vmem_limit_bytes=50 * 2**20
        ),
        cost_estimate=pl.CostEstimate(flops=14 * 10**9, bytes_accessed=13 * 2**20, transcendentals=0),
    )(tokens, out_grad, weight_codes, block_scales.T, proj_basis, first_prev.T, second_prev.T)
    ig, first, second, weight = pl.pallas_call(
        write_out,
        name="write_out",
        out_shape=(
            jax.ShapeDtypeStruct((TOK, D), BF16),
            jax.ShapeDtypeStruct((32, 1024), F32),
            jax.ShapeDtypeStruct((32, 1024), F32),
            jax.ShapeDtypeStruct((1024, N), BF16),
        ),
        in_specs=[vmem_spec] * 6,
        out_specs=(any_spec,) * 4,
        scratch_shapes=[pltpu.VMEM((512, 1024), BF16), pltpu.SemaphoreType.DMA((8,))],
        compiler_params=pltpu.CompilerParams(vmem_limit_bytes=16 * 2**20),
        cost_estimate=pl.CostEstimate(flops=10**9, bytes_accessed=14 * 2**20, transcendentals=0),
    )(*held, proj_basis)
    return ig, first.T, second.T, weight


def solution(mesh):
    in_specs = (
        P(("dp", "fsdp"), None),
        P(("dp", "fsdp"), None),
        P("fsdp", None),
        P("fsdp", None),
        P(),
        P("fsdp", "dp"),
        P("fsdp", "dp"),
    )
    out_specs = (P(("dp", "fsdp"), None), P("fsdp", "dp"), P("fsdp", "dp"), P("fsdp", None))
    return jax.shard_map(shards, mesh=mesh, in_specs=in_specs, out_specs=out_specs, check_vma=False)
```

```python
import math

import jax
import jax.numpy as jnp
from jax import lax
from jax.experimental import pallas as pl
from jax.experimental.pallas import tpu as pltpu
from jax.sharding import PartitionSpec as P

MESH = pl.DeviceIdType.MESH
BF16 = jnp.bfloat16
F32 = jnp.float32
beta_one = 0.9
beta_two = 0.999
learn_rate = 0.2
epsilon = 1e-08

D = 8192
N = 1024
RANK = 512
TOK = 512
OWN = 3
CHUNKS = ((1, 0, 1024), (2, 0, 1024), (3, 0, 1024), (0, 0, 512), (0, 512, 512))
OWN_AT = 3
ORDER = (
    ("P", 0), ("W0b",), ("P", 1), ("P", 2), ("C", 1), ("C", 0), ("P", 3), ("P", 4), ("E", 0), ("C", 2), ("Fxc0", 0),
    ("Fxc0", 3), ("P", 5), ("Fxc0", 1), ("C", 3), ("R", 0), ("C", 4), ("P", 6), ("Fzm", 2), ("P", 7), ("Fxc0", 2),
    ("C", 5), ("E", 3), ("Fzp", 1), ("R", 2), ("Y", 0), ("C", 7), ("Fo3", 0), ("P", 8), ("R", 3), ("Fo1", 3),
    ("Fxc1", 2), ("C", 6), ("E", 2), ("R", 4), ("R", 1), ("Fzm", 1), ("E", 4), ("C", 8), ("M", 0, 1, 0), ("Fxc3", 1),
    ("M", 3, 0, 0), ("R", 7), ("M", 0, 1, 1), ("M", 1, 0, 1), ("Fzm", 0), ("R", 5), ("Y", 3), ("M", 1, 0, 0),
    ("P", 9), ("Y", 2), ("E", 1), ("Fxc1", 1), ("E", 5), ("D2",), ("Fxc1", 0), ("E", 7), ("R", 6), ("R", 8), ("C", 9),
    ("F2", 1), ("M", 3, 0, 1), ("Y", 4), ("E", 6), ("X", 1), ("Y", 1), ("F2", 2), ("Fr1", 3), ("E", 9), ("Fzp", 3),
    ("E", 8), ("Fxc2", 1), ("Fr3", 0), ("M", 1, 1, 0), ("Y", 5), ("Fxc2", 2), ("X", 0), ("R", 9), ("Y", 6),
    ("Fyw", 1), ("Y", 8), ("Fzp", 2), ("Y", 7), ("Fyw", 3), ("Fzp", 0), ("X", 2), ("M", 3, 1, 0), ("Fzm", 3),
    ("Fyw", 0), ("Y", 9), ("Fyw", 2), ("Fxc3", 3), ("M", 0, 0, 0), ("X", 3), ("U", 0), ("X", 4), ("M", 1, 1, 1),
    ("U", 1), ("Fxc3", 2), ("M", 0, 0, 1), ("T", 0), ("M", 2, 1, 1), ("T", 1), ("M", 2, 0, 0), ("M", 2, 1, 0),
    ("M", 2, 0, 1), ("S", 0), ("M", 3, 1, 1), ("S", 1),
)
NT = (((1,), (1,)), ((), ()))
TN = (((0,), (1,)), ((), ()))


class Net:
    def __init__(self, send_sems, recv_sems, rows):
        self.send_sems, self.recv_sems, self.rows = send_sems, recv_sems, rows
        self.sems, self.got, self.sent = {}, set(), [0]

    def start(self, name, src, dst, device):
        size = math.prod(dst.shape) // N
        if self.sent[-1] + size > self.rows.shape[0]:
            self.sent.append(0)
        self.sent[-1] += size
        at, copies = self.sems.setdefault(name, (len(self.sems), []))
        copy = pltpu.make_async_remote_copy(
            src_ref=src,
            dst_ref=dst,
            send_sem=self.send_sems.at[len(self.sent) - 1],
            recv_sem=self.recv_sems.at[at],
            device_id=device,
            device_id_type=MESH,
        )
        copy.start()
        copies.append(size)

    def recv(self, name):
        if name not in self.got:
            self.got.add(name)
            at, copies = self.sems[name]
            whole = self.rows.at[: sum(copies)]
            pltpu.make_async_copy(whole, whole, self.recv_sems.at[at]).wait()

    def finish(self):
        for name in self.sems:
            self.recv(name)
        for at, size in enumerate(self.sent):
            whole = self.rows.at[:size]
            pltpu.make_async_copy(whole, whole, self.send_sems.at[at]).wait()


RECV_SEMS = 86
SEND_SEMS = 3


def update_rows(rows, step_all, basis, weight, out):
    step = step_all[:, :, :, rows].reshape(RANK, 512)
    change = lax.dot_general(step, basis[...], TN, preferred_element_type=F32)
    out[0:512, :] = (weight[rows, :].astype(F32) - learn_rate * change).astype(BF16)


def exchange(
    tokens, out_grad, codes, scales, basis, first_prev, second_prev,
    ig, step_all, first_new, second_new, weight,
    W, og, stage, cod, sca, bas, tok, proj_t, sib_out, sib_in, own, cs, rr, s2, y_in, cs2, x_in, low, z_out, z_in,
    fp, sp, send_sems, recv_sems, load_sems,
):
    d = lax.axis_index("dp")
    f = lax.axis_index("fsdp")
    xlo, y, c = d // 8, (d // 2) % 4, d % 2
    z, xhi = f // 2, f % 2

    def dev(dx=0, dh=0, dy=0, dz=0, dc=0):
        xl = 1 - xlo if dx else xlo
        xh = 1 - xhi if dh else xhi
        cc = 1 - c if dc else c
        return (xl * 8 + ((y + dy) % 4) * 2 + cc, ((z + dz) % 4) * 2 + xh)

    sib = dev(dc=1)
    zp, zm = dev(dz=1), dev(dz=3)
    yp, ym = dev(dy=1), dev(dy=3)
    xc, xs, xo = dev(dx=1, dh=1), dev(dx=1), dev(dh=1)
    peers = [sib, zp, zm, dev(dz=2), xc, xs, xo] + [dev(dx=j // 4, dy=j % 4) for j in (1, 2, 3, 5, 6, 7)]

    loads = {}

    def load(name, src, dst):
        copy = pltpu.make_async_copy(src, dst, load_sems.at[len(loads)])
        loads[name] = copy
        copy.start()

    half = pl.multiple_of(c * 512, 512)
    other = pl.multiple_of(512 - c * 512, 512)

    def load_codes(name, first, size):
        rows = pl.ds(pl.multiple_of(half + first, 128), size)
        load(name, codes.at[rows], cod.at[rows])

    load("scales", scales, sca)
    load_codes("codes_0", 0, 128)
    load_codes("codes_3", 384, 128)
    load("og", out_grad, og.at[0])
    load("basis", basis, bas)

    def part(q):
        dz, at, width = CHUNKS[q // 2]
        h = 1 - q % 2
        return dz, h, ((dz + 3) % 4) * 2 + h, slice(at, at + width), width

    def load_tokens(q):
        dz, h, _, cols, width = part(q)
        at = (((z + dz) % 4) * 2 + (1 - xhi if h else xhi)) * 1024 + cols.start
        src = tokens.at[:, pl.ds(pl.multiple_of(at, 512), width)]
        load(("tok", q), src, tok.at[q % 4, :, :width])

    load_tokens(0)
    load_codes("codes_12", 128, 256)

    barrier = pltpu.get_barrier_semaphore()
    for peer in peers:
        pl.semaphore_signal(barrier, inc=1, device_id=peer, device_id_type=MESH)

    def dequantize(base, tiles, also):
        for i in tiles:
            rows = pl.ds(pl.multiple_of(base + i * 128, 128), 128)
            s = jnp.transpose(sca[:, rows])
            for g in range(8):
                cols = slice(g * 128, (g + 1) * 128)
                w = (cod[rows, cols].astype(F32) * s[:, g : g + 1]).astype(BF16)
                weight[rows, cols] = w
                if also:
                    W[i * 128 : (i + 1) * 128, cols] = w

    loads["scales"].wait()
    loads["codes_0"].wait()
    loads["codes_3"].wait()
    dequantize(half, (0, 3), True)
    pl.semaphore_wait(barrier, len(peers))
    net = Net(send_sems, recv_sems, W)

    def half_of(i, xl):
        return i * 128 + xl * 64

    def wsend(name, way, dz, h, start, size):
        device, to_dz, to_h = {
            "z+": (zp, (dz + 3) % 4, h),
            "z-": (zm, (dz + 1) % 4, h),
            "xc": (xc, dz, 1 - h),
            "xs": (xs, dz, h),
            "y+": (yp, dz, h),
            "y-": (ym, dz, h),
        }[way]
        src, dst = ((dz * 2 + h) * 512 + start, (to_dz * 2 + to_h) * 512 + start)
        if not isinstance(start, int):
            src, dst = pl.multiple_of(src, 32), pl.multiple_of(dst, 32)
        net.start(name, W.at[pl.ds(src, size)], W.at[pl.ds(dst, size)], device)

    wsend(("zp", 0), "z+", 0, 0, 0, 128)
    wsend(("zm", 3), "z-", 0, 0, 384, 128)
    wsend(("xc0", 0), "xc", 0, 0, half_of(0, xlo), 64)
    wsend(("xc0", 3), "xc", 0, 0, half_of(3, xlo), 64)
    load_tokens(1)

    loads["og"].wait()
    loads["basis"].wait()
    projected = jnp.dot(og[0], bas[...], preferred_element_type=F32).astype(BF16)
    turned = jnp.transpose(projected)
    for j in range(16):
        jx, jy, jc = j // 8, (j // 2) % 4, j % 2
        row = jnp.where(c == jc, 0, 256) + ((jy - y + 4) % 4) * 64 + jx * 32
        proj_t[pl.ds(pl.multiple_of(row, 32), 32), :] = turned[j * 32 : (j + 1) * 32, :]

    def multiply(q):
        _, _, slot, span, width = part(q)
        loads["tok", q].wait()

        for i in range(0, width, 256):
            acc = jnp.dot(proj_t[...], tok[q % 4, :, i : i + 256], preferred_element_type=F32)
            own[q % OWN, :, i : i + 256] = acc[:256]
            sib_out[slot, :, span.start + i : span.start + i + 256] = acc[256:].astype(BF16)
        if 0 < q < 2 * len(CHUNKS) - 4:
            load_tokens(q + 4)

    def P(q):
        _, _, slot, cols, _ = part(q)
        multiply(q)
        if q == 0:
            net.start(("og",), og.at[0], og.at[1], sib)
            for later in (2, 3, 4):
                load_tokens(later)
            load("other_codes", codes.at[pl.ds(other, 512)], cod.at[pl.ds(other, 512)])
            load("fp", first_prev, fp)
            load("sp", second_prev, sp)
        net.start(("sib", q), sib_out.at[slot, :, cols], sib_in.at[slot, :, cols], sib)

    def C(q):
        _, h, slot, cols, width = part(q)
        net.recv(("sib", q))

        def tile(i, carry):
            rows = pl.ds(pl.multiple_of(i * 64, 64), 64)
            total = own[q % OWN, rows, :width] + sib_in[slot, rows, cols].astype(F32)
            cs[slot, rows, cols] = total.astype(BF16)
            return carry

        lax.fori_loop(0, 4, tile, 0)
        net.start(("far", q), cs.at[slot, 128:192, cols], rr.at[slot, :, cols], yp if h else ym)

    def E(q):
        _, h, slot, cols, _ = part(q)
        rows = slice(192, 256) if h else slice(64, 128)
        net.start(("y", q), cs.at[slot, rows, cols], y_in.at[slot, h, :, cols], ym if h else yp)

    def R(q):
        _, h, slot, cols, _ = part(q)
        net.recv(("far", q))
        rows = slice(64, 128) if h else slice(192, 256)
        s2[slot, :, cols] = (cs[slot, rows, cols].astype(F32) + rr[slot, :, cols].astype(F32)).astype(BF16)
        net.start(("y", q), s2.at[slot, :, cols], y_in.at[slot, 1 - h, :, cols], yp if h else ym)

    def Y(q):
        _, h, slot, cols, _ = part(q)
        net.recv(("y", q))
        total = cs[slot, 0:64, cols].astype(F32) + y_in[slot, 0, :, cols].astype(F32)
        cs2[slot, :, cols] = (total + y_in[slot, 1, :, cols].astype(F32)).astype(BF16)
        for n, to, xl in ((0, xc, 1 - xlo), (2, xo, xlo)) if h else ((1, xs, 1 - xlo),):
            rows = pl.ds(pl.multiple_of(xl * 32, 32), 32)
            net.start(("x", q // 2), cs2.at[slot, rows, cols], x_in.at[slot // 2, n, :, cols], to)

    def X(k):
        dz, _, slot, cols, _ = part(2 * k + 1)
        total = cs2[slot, pl.ds(pl.multiple_of(xlo * 32, 32), 32), cols].astype(F32)
        net.recv(("x", k))
        for n in range(3):
            total = total + x_in[slot // 2, n, :, cols].astype(F32)
        if dz == 0:
            low[:, cols] = total
        else:
            z_out[dz - 1] = total.astype(BF16)
            net.start(("z",), z_out.at[dz - 1], z_in.at[dz - 1], dev(dz=dz))

    def U(j):
        cols = part(2 * OWN_AT + 2 * j)[3]
        total = low[:, cols]
        net.recv(("z",))
        for dz in (1, 2, 3):
            total = total + z_in[dz - 1, :, cols].astype(F32)
        for name in ("fp", "sp"):
            if name in loads:
                loads.pop(name).wait()
        first = beta_one * fp[:, cols] + (1.0 - beta_one) * total
        second = beta_two * sp[:, cols] + (1.0 - beta_two) * total * total
        first_new[:, cols] = first
        second_new[:, cols] = second
        step_all[xlo * 4 + y, c, :, cols] = (first / (jnp.sqrt(second) + epsilon)).astype(BF16)
        mine = step_all.at[xlo * 4 + y, c, :, cols]
        net.start(("sx", j), mine, mine, xs)
        for i in (1, 3, 2):
            net.start(("step", j), mine, mine, dev(dy=i))

    def T(j):
        cols = part(2 * OWN_AT + 2 * j)[3]
        net.recv(("sx", j))
        theirs = step_all.at[(1 - xlo) * 4 + y, c, :, cols]
        for i in (1, 3, 2):
            net.start(("step", j), theirs, theirs, dev(dy=i))

    def S(j):
        cols = part(2 * OWN_AT + 2 * j)[3]
        net.recv(("step", j))
        ours = step_all.at[:, c, :, cols]
        net.start(("ss", j), ours, ours, sib)

    def D2():
        loads["other_codes"].wait()
        dequantize(other, range(4), False)

    def Fzp(i):
        net.recv(("zp", i))
        if i < 2:
            wsend(("zpp", i), "z+", 3, 0, i * 128, 128)
        if i != 0:
            wsend(("xc3", i), "xc", 3, 0, half_of(i, xlo), 64)

    def Fzm(i):
        net.recv(("zm", i))
        if i >= 2:
            wsend(("zmm", i), "z-", 1, 0, i * 128, 128)
        if i != 3:
            wsend(("xc1", i), "xc", 1, 0, half_of(i, xlo), 64)

    def forward_x(dz):
        def run(i):
            net.recv(("xc%d" % dz, i))
            wsend(("xs%d" % dz, i), "xs", dz, 1, half_of(i, 1 - xlo), 64)

        return run

    def Fo3(i):
        net.recv(("xc0", i))
        net.recv(("xs0", i))
        wsend(("zo3", i), "z+", 0, 1, i * 128, 128)

    def Fo1(i):
        net.recv(("xc0", i))
        net.recv(("xs0", i))
        wsend(("zo1", i), "z-", 0, 1, i * 128, 128)

    parity = y % 2

    def Fr3(i):
        net.recv(("zo3", i))
        wsend(("zr3", i), "z+", 3, 1, half_of(i, parity), 64)

    def Fr1(i):
        net.recv(("zo1", i))
        wsend(("zr1", i), "z-", 1, 1, half_of(i, parity), 64)

    def F2(i):
        net.recv(("zpp", i) if i < 2 else ("zmm", i))
        wsend(("xc2", i), "xc", 2, 0, half_of(i, parity) + xlo * 32, 32)

    def Fxc2(i):
        net.recv(("xc2", i))
        wsend(("xs2", i), "xs", 2, 1, half_of(i, parity) + (1 - xlo) * 32, 32)

    def Fyw(i):
        if i in (0, 3):
            net.recv(("zr%d" % (1 if i else 3), i))
        else:
            net.recv(("xc2", i))
            net.recv(("xs2", i))
        wsend(("yw", i // 2), "y+" if i < 2 else "y-", 2, 1, half_of(i, parity), 64)

    def M(dz, h, u):
        for i in (2 * u, 2 * u + 1):
            if h == 0:
                if dz:
                    net.recv((None, "zm", "zpp" if i < 2 else "zmm", "zp")[dz : dz + 1] + (i,))
            elif (dz, i) in ((3, 0), (1, 3)):
                net.recv(("zo%d" % dz, i))
            elif dz == 2 and i in (0, 3):
                net.recv(("zr%d" % (1 if i else 3), i))
            else:
                net.recv(("xc%d" % dz, i))
                net.recv(("xs%d" % dz, i))
            if (dz, h) == (2, 1):
                net.recv(("yw", u))
        net.recv(("og",))
        slot = dz * 2 + h
        fsdp = ((z + dz) % 4) * 2 + (1 - xhi if h else xhi)
        cols = pl.ds(pl.multiple_of(fsdp * 1024 + c * 512 + u * 256, 256), 256)

        at = slot * 512 + u * 256

        def tile(i, carry):
            rows = pl.ds(pl.multiple_of(i * 256, 256), 256)
            w = W[at : at + 256, :]
            theirs = lax.dot_general(og[1, rows, :], w, NT, preferred_element_type=F32)
            stage[slot, u, rows, :] = theirs.astype(BF16)
            mine = lax.dot_general(og[0, rows, :], w, NT, preferred_element_type=F32)
            ig[rows, cols] = mine.astype(BF16)
            return carry

        lax.fori_loop(0, 2, tile, 0)
        net.start(("ig",), stage.at[slot, u], ig.at[:, cols], sib)

    def W0b():
        loads["codes_12"].wait()
        dequantize(half, (1, 2), True)
        wsend(("zp", 1), "z+", 0, 0, 128, 128)
        wsend(("zm", 2), "z-", 0, 0, 256, 128)
        wsend(("xc0", 1), "xc", 0, 0, half_of(1, xlo), 64)
        wsend(("xc0", 2), "xc", 0, 0, half_of(2, xlo), 64)
        wsend(("zp", 2), "z+", 0, 0, 256, 128)
        wsend(("zm", 1), "z-", 0, 0, 128, 128)
        wsend(("zp", 3), "z+", 0, 0, 384, 128)
        wsend(("zm", 0), "z-", 0, 0, 0, 128)

    steps = dict(
        W0b=W0b, Fyw=Fyw,
        P=P, C=C, E=E, R=R, Y=Y, X=X, U=U, T=T, S=S, M=M, D2=D2, Fzp=Fzp, Fzm=Fzm, Fo3=Fo3, Fo1=Fo1, Fr3=Fr3,
        Fr1=Fr1, F2=F2, Fxc0=forward_x(0), Fxc1=forward_x(1), Fxc2=Fxc2, Fxc3=forward_x(3),
    )
    for name, *place in ORDER:
        steps[name](*place)

    net.recv(("ss", 0))
    update_rows(slice(0, 512), step_all, bas, weight, weight)
    net.finish()


def write_out(ig, step_all, first_new, second_new, weight, basis, ig_out, first_out, second_out, weight_out, nw, sems):
    copies = [
        pltpu.make_async_copy(ig.at[pl.ds(i * 128, 128)], ig_out.at[pl.ds(i * 128, 128)], sems.at[i]) for i in range(4)
    ]
    copies.append(pltpu.make_async_copy(first_new, first_out, sems.at[4]))
    copies.append(pltpu.make_async_copy(second_new, second_out, sems.at[5]))
    copies.append(pltpu.make_async_copy(weight.at[pl.ds(0, 512)], weight_out.at[pl.ds(0, 512)], sems.at[6]))
    for copy in copies:
        copy.start()
    update_rows(slice(512, 1024), step_all, basis, weight, nw)
    copy = pltpu.make_async_copy(nw, weight_out.at[pl.ds(512, 512)], sems.at[7])
    copy.start()
    copies.append(copy)
    for copy in copies:
        copy.wait()


def shards(tokens, out_grad, weight_codes, block_scales, proj_basis, first_prev, second_prev):
    any_spec = pl.BlockSpec(memory_space=pl.ANY)
    vmem_spec = pl.BlockSpec(memory_space=pltpu.VMEM)
    held = pl.pallas_call(
        exchange,
        name="exchange",
        out_shape=(
            pltpu.VMEM((TOK, D), BF16),
            pltpu.VMEM((8, 2, 32, 1024), BF16),
            pltpu.VMEM((32, 1024), F32),
            pltpu.VMEM((32, 1024), F32),
            pltpu.VMEM((1024, N), BF16),
        ),
        in_specs=[any_spec] * 7,
        out_specs=(vmem_spec,) * 5,
        scratch_shapes=[
            pltpu.VMEM((4096, 1024), BF16),
            pltpu.VMEM((2, 512, 1024), BF16),
            pltpu.VMEM((8, 2, 512, 256), BF16),
            pltpu.VMEM((1024, 1024), BF16),
            pltpu.VMEM((8, 1024), F32),
            pltpu.VMEM((1024, 512), BF16),
            pltpu.VMEM((4, 512, 1024), BF16),
            pltpu.VMEM((512, 512), BF16),
            pltpu.VMEM((8, 256, 1024), BF16),
            pltpu.VMEM((8, 256, 1024), BF16),
            pltpu.VMEM((OWN, 256, 1024), F32),
            pltpu.VMEM((8, 256, 1024), BF16),
            pltpu.VMEM((8, 64, 1024), BF16),
            pltpu.VMEM((8, 64, 1024), BF16),
            pltpu.VMEM((8, 2, 64, 1024), BF16),
            pltpu.VMEM((8, 64, 1024), BF16),
            pltpu.VMEM((4, 3, 32, 1024), BF16),
            pltpu.VMEM((32, 1024), F32),
            pltpu.VMEM((3, 32, 1024), BF16),
            pltpu.VMEM((3, 32, 1024), BF16),
            pltpu.VMEM((32, 1024), F32),
            pltpu.VMEM((32, 1024), F32),
            pltpu.SemaphoreType.DMA((SEND_SEMS,)),
            pltpu.SemaphoreType.DMA((RECV_SEMS,)),
            pltpu.SemaphoreType.DMA((19,)),
        ],
        compiler_params=pltpu.CompilerParams(
            collective_id=0, has_side_effects=True, vmem_limit_bytes=50 * 2**20
        ),
        cost_estimate=pl.CostEstimate(flops=14 * 10**9, bytes_accessed=13 * 2**20, transcendentals=0),
    )(tokens, out_grad, weight_codes, block_scales.T, proj_basis, first_prev.T, second_prev.T)
    ig, first, second, weight = pl.pallas_call(
        write_out,
        name="write_out",
        out_shape=(
            jax.ShapeDtypeStruct((TOK, D), BF16),
            jax.ShapeDtypeStruct((32, 1024), F32),
            jax.ShapeDtypeStruct((32, 1024), F32),
            jax.ShapeDtypeStruct((1024, N), BF16),
        ),
        in_specs=[vmem_spec] * 6,
        out_specs=(any_spec,) * 4,
        scratch_shapes=[pltpu.VMEM((512, 1024), BF16), pltpu.SemaphoreType.DMA((8,))],
        compiler_params=pltpu.CompilerParams(vmem_limit_bytes=16 * 2**20),
        cost_estimate=pl.CostEstimate(flops=10**9, bytes_accessed=14 * 2**20, transcendentals=0),
    )(*held, proj_basis)
    return ig, first.T, second.T, weight


def solution(mesh):
    in_specs = (
        P(("dp", "fsdp"), None),
        P(("dp", "fsdp"), None),
        P("fsdp", None),
        P("fsdp", None),
        P(),
        P("fsdp", "dp"),
        P("fsdp", "dp"),
    )
    out_specs = (P(("dp", "fsdp"), None), P("fsdp", "dp"), P("fsdp", "dp"), P("fsdp", None))
    return jax.shard_map(shards, mesh=mesh, in_specs=in_specs, out_specs=out_specs, check_vma=False)
```
